32 devices in a mesh: sys: 2 (over x), row: 4 (over y, core), col: 4 (over z).
Axes of the slice: x: 2, y: 2, z: 4, core: 2. Of those that a mesh axis runs over, the one named last changes fastest.
Arguments:
- density: bfloat16 [4, 4, 8, 19, 128, 128], P('row', 'col', 'sys'), parts along dimension 2, may hold values from -0.5 to 0.5, as said below
- neighbours: int32 [4, 4, 8, 19], P('row', 'col', 'sys'), parts along dimension 2, may hold values from -1 to 63, as said below
- square_pattern: int32 [4, 4, 4, 50], P('row', 'col', 'sys'), parts along dimension 2, may hold values from -1 to 63, as said below
Outputs:
- purified: bfloat16 [4, 4, 4, 19, 128, 128], P('row', 'col', 'sys'), parts along dimension 2
The draws below stay inside these ranges and needn't reach their ends.
There are 2 independent parts, one for each index of `sys`. The reference program is written for one: setup_inputs(seed, part) draws one part's arguments, and reference() takes and returns one part's arrays. A program takes and returns all parts, laid end to end along the dimension named above; each array names one. Nothing has to cross between parts.
Inputs may be any that keep to these rules, and one draw needn't show every extreme that they name: `density`: block w of row g holds the block of P at (g, neighbours[g, w]); the block at (j, g) is the transpose of the one at (g, j), and slots whose neighbour is -1 hold zeros. `neighbours`: row g of the whole array lists, in any order and each once, the groups j whose block P[g, j] is stored, g itself always among them, with -1 in the unused slots; j is listed in row g exactly when g is listed in row j. Group g belongs to the device at row index g // 16 and col index (g // 4) % 4, as its plane g % 4; every listed group belongs to that same device or to one of the eight devices next to it along row, col or both, and a listed group of a device that differs along both row and col has the same plane as g. `square_pattern`: row l of a device lists, in any order and each once, with -1 in the unused slots, groups m for which some group k is listed in the neighbours row of that device's plane l + 1 and m is listed in the neighbours row of k: the blocks of the square kept after filtering, all of them where there are at most 50.
All inputs are finite; a program needn't handle non-finite values.
Results may differ from the reference program's by a relative error of at most 0.0038.
Values may be sent and summed in bfloat16 or wider, within the bound.
A program may use at most 128 MiB of HBM per device.

```python
import jax
import jax.numpy as jnp
import numpy as np
from jax import lax

B = 128
W = 19
LAYERS = 2
DEPTH = 4
W2 = 50
GROUPS = 64
N_ROW = 4
N_COL = 4


def shell_offsets():
    listed = [(step_one, step_two, step_three) for step_one in (-1, 0, 1) for step_two in (-1, 0, 1) for step_three in (-1, 0, 1) if step_one * step_one + step_two * step_two + step_three * step_three <= 2]
    return np.array(listed, np.int32)


def paired_offsets():
    shells = shell_offsets()
    joined = sorted({(int(left_part[0] + right_part[0]), int(left_part[1] + right_part[1]), int(left_part[2] + right_part[2])) for left_part in shells for right_part in shells})
    return np.array(joined, np.int32)


def lattice_lists(offsets):
    group_ids = jnp.arange(N_ROW * N_COL * DEPTH, dtype=jnp.int32)
    first_pos = group_ids // (N_COL * DEPTH)
    second_pos = group_ids // DEPTH % N_COL
    third_pos = group_ids % DEPTH
    shifts = jnp.asarray(offsets)
    moved_first = first_pos[:, None] + shifts[None, :, 0]
    moved_second = second_pos[:, None] + shifts[None, :, 1]
    moved_third = third_pos[:, None] + shifts[None, :, 2]
    inside = (moved_first >= 0) & (moved_first < N_ROW) & (moved_second >= 0) & (moved_second < N_COL) & (moved_third >= 0) & (moved_third < DEPTH)
    return jnp.where(inside, (moved_first * N_COL + moved_second) * DEPTH + moved_third, -1).astype(jnp.int32)


def neighbour_table(key):
    lattice_table = lattice_lists(shell_offsets())
    salted = jax.random.fold_in(key, 11)
    scores = jax.random.randint(salted, lattice_table.shape, 0, 4096, dtype=jnp.int32) * 32 + lax.broadcasted_iota(jnp.int32, lattice_table.shape, 1)
    ranking = jnp.argsort(scores, axis=1, stable=True)
    return jnp.take_along_axis(lattice_table, ranking, axis=1)


def draw_neighbours(key, part):
    return neighbour_table(key).reshape(N_ROW, N_COL, DEPTH, W)


def draw_density(key, part):
    lattice_table = neighbour_table(key)
    key = jax.random.fold_in(key, 5)
    group_ids = jnp.arange(GROUPS, dtype=jnp.int32)[:, None]
    lower_id = jnp.minimum(group_ids, lattice_table)
    upper_id = jnp.maximum(group_ids, lattice_table)
    pair_ids = jnp.maximum(lower_id, 0) * GROUPS + upper_id
    subkeys = jax.vmap(jax.vmap(lambda pair_index: jax.random.fold_in(key, pair_index)))(pair_ids)
    samples = jax.vmap(jax.vmap(lambda subkey: jax.random.truncated_normal(subkey, -3.0, 3.0, (B, B), jnp.float32)))(subkeys)
    flipped = jnp.swapaxes(samples, 2, 3)
    below_diag = (group_ids > lattice_table)[:, :, None, None]
    itself = (group_ids == lattice_table)[:, :, None, None]
    present = (lattice_table >= 0)[:, :, None, None]
    blocks = jnp.where(below_diag, flipped, samples)
    blocks = jnp.where(itself, 0.5 * (samples + flipped), blocks)
    blocks = jnp.where(present, blocks, 0.0) * (W * B) ** (-1.0 / 3.0)
    return blocks.astype(jnp.bfloat16).reshape(N_ROW, N_COL, DEPTH, W, B, B)


def draw_square_pattern(key, part):
    key = jax.random.fold_in(key, 23)
    lattice_table = lattice_lists(paired_offsets())
    offset_count = lattice_table.shape[-1]
    lattice_table = lattice_table.reshape(N_ROW, N_COL, DEPTH, offset_count)[:, :, 1:DEPTH - 1].reshape(-1, offset_count)
    scores = jax.random.randint(key, lattice_table.shape, 0, 4096, dtype=jnp.int32) * 128 + lax.broadcasted_iota(jnp.int32, lattice_table.shape, 1)
    scores = jnp.where(lattice_table >= 0, scores, scores + (1 << 24))
    ranking = jnp.argsort(scores, axis=1, stable=True)
    chosen_ids = jnp.take_along_axis(lattice_table, ranking, axis=1)[:, :W2]
    second = jax.random.randint(jax.random.fold_in(key, 1), chosen_ids.shape, 0, 4096, dtype=jnp.int32) * 128 + lax.broadcasted_iota(jnp.int32, chosen_ids.shape, 1)
    chosen_ids = jnp.take_along_axis(chosen_ids, jnp.argsort(second, axis=1, stable=True), axis=1)
    return chosen_ids.reshape(N_ROW, N_COL, LAYERS, W2)


def setup_inputs(seed: int = 0, part: int = 0) -> dict:
    arg_keys = jax.random.split(jax.random.key(seed), 4)
    part_keys = jax.random.split(jax.random.fold_in(arg_keys[3], part), 4)
    density = draw_density(jax.random.fold_in(jax.random.fold_in(arg_keys[3], part), 71), part)
    neighbours = draw_neighbours(jax.random.fold_in(jax.random.fold_in(arg_keys[3], part), 71), part)
    square_pattern = draw_square_pattern(jax.random.fold_in(jax.random.fold_in(arg_keys[3], part), 71), part)
    return {"density": density, "neighbours": neighbours, "square_pattern": square_pattern}


def find_slots(wanted, listed):
    slot_count = listed.shape[-1]
    matches = (wanted[..., None] == listed) & (wanted[..., None] >= 0)
    places = jnp.sum(jnp.where(matches, jnp.arange(slot_count, dtype=jnp.int32), 0), axis=-1).astype(jnp.int32)
    return jnp.where(jnp.any(matches, axis=-1), places, slot_count).astype(jnp.int32)


def reference(density, neighbours, square_pattern):
    rows_first, rows_second, plane_count, slot_count, block_size, _ = density.shape
    layer_count, square_slots = square_pattern.shape[2], square_pattern.shape[3]
    group_total = rows_first * rows_second * plane_count
    blocks = density.reshape(group_total, slot_count, block_size, block_size)
    columns = neighbours.reshape(group_total, slot_count)
    purified_rows = (jnp.arange(rows_first * rows_second, dtype=jnp.int32)[:, None] * plane_count + 1 + jnp.arange(layer_count, dtype=jnp.int32)[None, :]).reshape(-1)
    listed = square_pattern.reshape(-1, square_slots)

    def one_row(inputs):
        group, list_two = inputs
        own_blocks = blocks[group].astype(jnp.float32)
        own_cols = columns[group]
        present = own_cols >= 0
        clamped = jnp.where(present, own_cols, group).astype(jnp.int32)
        near_rows = blocks[clamped].astype(jnp.float32)
        near_cols = columns[clamped]
        both_live = present[:, None] & (near_cols >= 0)
        target = jnp.where(both_live, find_slots(near_cols, list_two), square_slots).astype(jnp.int32)
        products = jnp.einsum("kab,kwbc->kwac", own_blocks, near_rows)
        summed = jax.ops.segment_sum(products.reshape(slot_count * slot_count, block_size, block_size), target.reshape(-1), num_segments=square_slots + 1)
        square = summed[:square_slots].astype(jnp.bfloat16)
        padded = jnp.concatenate([square, jnp.zeros((1, block_size, block_size), jnp.bfloat16)], axis=0)
        chosen = jnp.where(near_cols >= 0, find_slots(near_cols, list_two), square_slots).astype(jnp.int32)
        cubed = jnp.einsum("jwab,jwcb->jac", padded[chosen].astype(jnp.float32), near_rows)
        own_place = jnp.where(present, find_slots(own_cols, list_two), square_slots).astype(jnp.int32)
        updated = 3.0 * padded[own_place].astype(jnp.float32) - 2.0 * cubed
        return jnp.where(present[:, None, None], updated, 0.0).astype(jnp.bfloat16)

    result = lax.map(one_row, (purified_rows, listed))
    return result.reshape(rows_first, rows_second, layer_count, slot_count, block_size, block_size)
```

```python
import functools

import jax
import jax.numpy as jnp
from jax import lax
from jax.experimental import pallas as pl
from jax.experimental.pallas import tpu as pltpu
from jax.sharding import PartitionSpec as P

PLUS = ((-1, 0), (0, -1), (0, 0), (0, 1), (1, 0))
DIAG = ((-1, -1), (-1, 1), (1, -1), (1, 1))
DEPTH = 4
MESH = pl.DeviceIdType.MESH
NT = (((1,), (1,)), ((), ()))


def ext(a, b):
    return ((a + 2) * 5 + b + 2) * DEPTH


def near(a, b):
    return (a + 1) * 3 + b + 1


def plus_shift(d):
    x = d - 2
    return 2 * x + 2 * x * x * x


def dot(a, b):
    return jnp.dot(a, b, preferred_element_type=jnp.float32)


def dot_nt(a, b):
    return lax.dot_general(a, b, NT, preferred_element_type=jnp.float32)


def kernel(
    rows, cols, slots,
    dens, tab_v, tab_own, mask, place, square_place, live,
    out,
    own, row_lo, row_hi, mid_lo, mid_hi, end_lo, end_hi,
    diag_ll, diag_lh, diag_hl, diag_hh,
    tabs_v, tabs, lhs, acc, square, cubed,
    local_sem, tab_send, tab_recv, tab_local,
    row_send, row_recv, mid_send, mid_recv, end_send, end_recv, diag_send, diag_recv,
):
    r = lax.axis_index("row")
    c = lax.axis_index("col")
    size = own.shape[-1]
    row_bufs, mid_bufs, end_bufs = (row_lo, row_hi), (mid_lo, mid_hi), (end_lo, end_hi)
    diag_bufs = ((diag_ll, diag_lh), (diag_hl, diag_hh))

    def exists(a, b):
        here = None
        for step, at, count in ((a, r, rows), (b, c, cols)):
            test = at > 0 if step < 0 else at < count - 1
            if step:
                here = test if here is None else jnp.logical_and(here, test)
        return here

    def device(a, b):
        return {"row": r + a, "col": c + b}

    around = [s for s in PLUS + DIAG if s != (0, 0)]
    barrier = pltpu.get_barrier_semaphore()
    for a, b in around:
        @pl.when(exists(a, b))
        def _(a=a, b=b):
            pl.semaphore_signal(barrier, inc=1, device_id=device(a, b), device_id_type=MESH)
    high = (r + 1) // rows
    low = (rows - r) // rows
    right = (c + 1) // cols
    left = (cols - c) // cols
    pl.semaphore_wait(barrier, (3 - high - low) * (3 - right - left) - 1)

    def tab_copy(a, b):
        return pltpu.make_async_remote_copy(
            src_ref=tab_v, dst_ref=tabs_v.at[near(-a, -b)],
            send_sem=tab_send.at[near(a, b)], recv_sem=tab_recv.at[near(-a, -b)],
            device_id=device(a, b), device_id_type=MESH)

    def row_copy(side):
        return pltpu.make_async_remote_copy(
            src_ref=dens, dst_ref=row_bufs[side].at[:, pl.ds(0, slots)],
            send_sem=row_send.at[side], recv_sem=row_recv.at[side],
            device_id=device(1 - 2 * side, 0), device_id_type=MESH)

    def mid_copy(side, i):
        return pltpu.make_async_remote_copy(
            src_ref=dens.at[1 + i], dst_ref=mid_bufs[side].at[i, pl.ds(0, slots)],
            send_sem=mid_send.at[side, i], recv_sem=mid_recv.at[side, i],
            device_id=device(0, 1 - 2 * side), device_id_type=MESH)

    def end_copy(side, i):
        return pltpu.make_async_remote_copy(
            src_ref=dens.at[3 * i], dst_ref=end_bufs[side].at[i, pl.ds(0, slots)],
            send_sem=end_send.at[side, i], recv_sem=end_recv.at[side, i],
            device_id=device(0, 1 - 2 * side), device_id_type=MESH)

    def diag_copy(side, col_side, i):
        return pltpu.make_async_remote_copy(
            src_ref=mid_bufs[col_side].at[i, pl.ds(0, slots)],
            dst_ref=diag_bufs[side][col_side].at[i, pl.ds(0, slots)],
            send_sem=diag_send.at[side, col_side, i], recv_sem=diag_recv.at[side, col_side, i],
            device_id=device(1 - 2 * side, 0), device_id_type=MESH)

    sides = (0, 1)
    for a, b in around:
        pl.when(exists(a, b))(lambda a=a, b=b: tab_copy(a, b).start())
    for i in sides:
        for side in sides:
            pl.when(exists(0, 1 - 2 * side))(lambda side=side, i=i: mid_copy(side, i).start())
    for side in sides:
        pl.when(exists(1 - 2 * side, 0))(lambda side=side: row_copy(side).start())
    for i in sides:
        for side in sides:
            pl.when(exists(0, 1 - 2 * side))(lambda side=side, i=i: end_copy(side, i).start())
    load = pltpu.make_async_copy(dens, own.at[:, pl.ds(0, slots)], local_sem)
    load.start()

    blank = jnp.zeros((size, size), own.dtype)
    for buf in (own,) + row_bufs + mid_bufs + end_bufs + diag_bufs[0] + diag_bufs[1]:
        for i in range(buf.shape[0]):
            buf[i, slots] = blank

    @pl.loop(0, acc.shape[0])
    def _(e):
        acc[e] = jnp.zeros((2 * size, size), jnp.float32)

    for a, b in around:
        @pl.when(exists(a, b))
        def _(a=a, b=b):
            tab_copy(-a, -b).wait_recv()
            copy = pltpu.make_async_copy(
                tabs_v.at[near(a, b)], tabs.at[near(a, b)], tab_local.at[near(a, b)])
            copy.start()
            copy.wait()
    load.wait()

    def held(a, b, l, q):
        slot = tab_own[l, q] if (a, b) == (0, 0) else tabs[near(a, b), l, q]
        if (a, b) == (0, 0):
            return own[l, slot]
        if b == 0:
            return row_bufs[(a + 1) // 2][l, slot]
        if a == 0:
            if l in (1, 2):
                return mid_bufs[(b + 1) // 2][l - 1, slot]
            return end_bufs[(b + 1) // 2][l // 3, slot]
        return diag_bufs[(a + 1) // 2][(b + 1) // 2][l - 1, slot]

    planes = range(DEPTH)

    def add_plus(a, b):
        at = PLUS.index((a, b))
        for l in planes:
            for g in (0, 1):
                lhs[g * size:(g + 1) * size, l * size:(l + 1) * size] = own[
                    g + 1, tab_own[g + 1, at * DEPTH + l]]

        @pl.loop(0, len(PLUS))
        def _(d):
            right_side = jnp.concatenate([
                jnp.concatenate([held(a, b, l, d * DEPTH + p) for p in planes], axis=1)
                for l in planes], axis=0)
            total = dot(lhs[...], right_side)
            e = ext(a, b) + plus_shift(d)
            for p in planes:
                acc[e + p] += total[:, p * size:(p + 1) * size]

        for l in planes:
            right_side = jnp.concatenate(
                [held(a, b, l, len(PLUS) * DEPTH + i) for i in range(4)], axis=1)
            total = dot(lhs[:, l * size:(l + 1) * size], right_side)
            for i, (da, db) in enumerate(DIAG):
                acc[ext(a + da, b + db) + l] += total[:, i * size:(i + 1) * size]

    def add_diag(a, b):
        at = len(PLUS) * DEPTH + DIAG.index((a, b))
        for g in (0, 1):
            l = g + 1
            left_side = own[l, tab_own[l, at]]
            half = slice(g * size, (g + 1) * size)

            @pl.loop(0, len(PLUS))
            def _(d):
                right_side = jnp.concatenate(
                    [held(a, b, l, d * DEPTH + p) for p in planes], axis=1)
                total = dot(left_side, right_side)
                e = ext(a, b) + plus_shift(d)
                for p in planes:
                    acc[e + p, half] += total[:, p * size:(p + 1) * size]

            right_side = jnp.concatenate(
                [held(a, b, l, len(PLUS) * DEPTH + i) for i in range(4)], axis=1)
            total = dot(left_side, right_side)
            for i, (da, db) in enumerate(DIAG):
                acc[ext(a + da, b + db) + l, half] += total[:, i * size:(i + 1) * size]

    add_plus(0, 0)
    for i in sides:
        for col_side in sides:
            b = 2 * col_side - 1
            pl.when(exists(0, b))(lambda s=col_side, i=i: mid_copy(s, i).wait_recv())
            for side in sides:
                pl.when(jnp.logical_and(exists(0, b), exists(1 - 2 * side, 0)))(
                    lambda side=side, s=col_side, i=i: diag_copy(side, s, i).start())
    for side in sides:
        a = 2 * side - 1

        @pl.when(exists(a, 0))
        def _(a=a, side=side):
            row_copy(side).wait_recv()
            add_plus(a, 0)
    for side in sides:
        b = 2 * side - 1

        @pl.when(exists(0, b))
        def _(b=b, side=side):
            end_copy(side, 0).wait_recv()
            end_copy(side, 1).wait_recv()
            add_plus(0, b)
    for side in sides:
        for col_side in sides:
            a, b = 2 * side - 1, 2 * col_side - 1

            @pl.when(exists(a, b))
            def _(a=a, b=b, side=side, col_side=col_side):
                diag_copy(side, col_side, 0).wait_recv()
                diag_copy(side, col_side, 1).wait_recv()
                add_diag(a, b)

    @pl.loop(0, acc.shape[0])
    def _(e):
        for g in (0, 1):
            half = slice(g * size, (g + 1) * size)
            square[e, half] = jnp.where(mask[g, e] > 0, acc[e, half], 0.0).astype(square.dtype)

    def cube_plus(a, b):
        first = near(a, b) * DEPTH
        for l in planes:
            left_side = jnp.concatenate(
                [square[ext(a + da, b + db) + l] for da, db in DIAG], axis=1)
            right_side = jnp.concatenate(
                [held(a, b, l, len(PLUS) * DEPTH + i) for i in range(4)], axis=1)
            cubed[first + l] = dot_nt(left_side, right_side)

        @pl.loop(0, len(PLUS))
        def _(d):
            e = ext(a, b) + plus_shift(d)
            left_side = jnp.concatenate([square[e + p] for p in planes], axis=1)
            right_side = jnp.concatenate([
                jnp.concatenate([held(a, b, l, d * DEPTH + p) for p in planes], axis=1)
                for l in planes], axis=0)
            total = dot_nt(left_side, right_side)
            for l in planes:
                cubed[first + l] += total[:, l * size:(l + 1) * size]

    def cube_diag(a, b):
        for g in (0, 1):
            l = g + 1
            half = slice(g * size, (g + 1) * size)
            left_side = jnp.concatenate(
                [square[ext(a + da, b + db) + l, half] for da, db in DIAG]
                + [square[ext(a + da, b + db) + p, half] for da, db in PLUS for p in planes], axis=1)
            places = [len(PLUS) * DEPTH + i for i in range(4)] + list(range(len(PLUS) * DEPTH))
            right_side = jnp.concatenate([held(a, b, l, q) for q in places], axis=1)
            cubed[near(a, b) * DEPTH + l, half] = dot_nt(left_side, right_side)

    cube_plus(0, 0)
    for a, b in around:
        pl.when(exists(a, b))(
            lambda a=a, b=b: cube_diag(a, b) if a and b else cube_plus(a, b))

    @pl.loop(0, slots)
    def _(w):
        for g in (0, 1):
            half = slice(g * size, (g + 1) * size)
            updated = (3.0 * square[square_place[g, w], half].astype(jnp.float32)
                       - 2.0 * cubed[place[g, w], half])
            out[g, w] = jnp.where(live[g, w] > 0, updated, 0.0).astype(out.dtype)

    for a, b in around:
        pl.when(exists(a, b))(lambda a=a, b=b: tab_copy(a, b).wait_send())
    for side in sides:
        pl.when(exists(1 - 2 * side, 0))(lambda side=side: row_copy(side).wait_send())
        for i in sides:
            pl.when(exists(0, 1 - 2 * side))(lambda side=side, i=i: mid_copy(side, i).wait_send())
            pl.when(exists(0, 1 - 2 * side))(lambda side=side, i=i: end_copy(side, i).wait_send())
            for s in sides:
                pl.when(jnp.logical_and(exists(0, 2 * s - 1), exists(1 - 2 * side, 0)))(
                    lambda side=side, s=s, i=i: diag_copy(side, s, i).wait_send())


def shards(rows, cols, density, neighbours, square_pattern):
    density, neighbours, square_pattern = density[0, 0], neighbours[0, 0], square_pattern[0, 0]
    slots, size = density.shape[1], density.shape[2]
    here = (lax.axis_index("row"), lax.axis_index("col"))

    def steps(groups):
        cell = jnp.maximum(groups, 0) // DEPTH
        return cell // cols - here[0], cell % cols - here[1], jnp.maximum(groups, 0) % DEPTH

    da, db, p = steps(neighbours)
    present = neighbours >= 0
    side = 2 + db + 2 * da
    straight = (da * db) == 0
    q = jnp.where(straight, side * DEPTH + p, 20 + (da + 1) + (db + 1) // 2)
    hit = (q[..., None] == jnp.arange(24)) & present[..., None]
    slot_ids = jnp.arange(slots, dtype=jnp.int32)[None, :, None]
    table = slots - jnp.sum(jnp.where(hit, slots - slot_ids, 0), axis=1)
    table = jnp.pad(table.astype(jnp.int32), ((0, 4), (0, 104)), constant_values=slots)
    live = present[1:3].astype(jnp.int32)
    place = jnp.where(present, (near(da, db)) * DEPTH + p, 16)[1:3].astype(jnp.int32)
    square_place = jnp.where(present, ext(da, db) + p, ext(0, 0))[1:3].astype(jnp.int32)
    sa, sb, sp = steps(square_pattern)
    kept = jnp.where(square_pattern >= 0, ext(sa, sb) + sp, -1)
    mask = jnp.any(kept[..., None] == jnp.arange(100), axis=1).astype(jnp.int32)

    block = (size, size)
    dma = pltpu.SemaphoreType.DMA
    bf16 = density.dtype

    def buf(n):
        return pltpu.VMEM((n, slots + 1) + block, bf16)

    smem = pl.BlockSpec(memory_space=pltpu.SMEM)
    purified = pl.pallas_call(
        functools.partial(kernel, rows, cols, slots),
        out_shape=jax.ShapeDtypeStruct((2, slots) + block, bf16),
        in_specs=[pl.BlockSpec(memory_space=pl.ANY), pl.BlockSpec(memory_space=pltpu.VMEM)] + [smem] * 5,
        out_specs=pl.BlockSpec(memory_space=pltpu.VMEM),
        scratch_shapes=[
            buf(4), buf(4), buf(4), buf(2), buf(2), buf(2), buf(2), buf(2), buf(2), buf(2), buf(2),
            pltpu.VMEM((9, 8, 128), jnp.int32),
            pltpu.SMEM((9, 8, 128), jnp.int32),
            pltpu.VMEM((2 * size, DEPTH * size), bf16),
            pltpu.VMEM((100, 2 * size, size), jnp.float32),
            pltpu.VMEM((100, 2 * size, size), bf16),
            pltpu.VMEM((36, 2 * size, size), jnp.float32),
            dma, dma((9,)), dma((9,)), dma((9,)),
            dma((2,)), dma((2,)), dma((2, 2)), dma((2, 2)), dma((2, 2)), dma((2, 2)),
            dma((2, 2, 2)), dma((2, 2, 2)),
        ],
        compiler_params=pltpu.CompilerParams(
            collective_id=0, has_side_effects=True, vmem_limit_bytes=56 * 1024 * 1024),
        cost_estimate=pl.CostEstimate(flops=6 * 10**9, bytes_accessed=20 * 10**6, transcendentals=0),
    )(density, table, table, mask, place, square_place, live)
    return purified[None, None]


def solution(mesh):
    in_specs = (
        P("row", "col", "sys", None, None, None),
        P("row", "col", "sys", None),
        P("row", "col", "sys", None),
    )
    out_specs = P("row", "col", "sys", None, None, None)
    body = functools.partial(shards, mesh.shape["row"], mesh.shape["col"])
    return jax.shard_map(body, mesh=mesh, in_specs=in_specs, out_specs=out_specs, check_vma=False)
```

```python
import functools

import jax
import jax.numpy as jnp
from jax import lax
from jax.experimental import pallas as pl
from jax.experimental.pallas import tpu as pltpu
from jax.sharding import PartitionSpec as P

PLUS = ((-1, 0), (0, -1), (0, 0), (0, 1), (1, 0))
DIAG = ((-1, -1), (-1, 1), (1, -1), (1, 1))
DEPTH = 4
UNROLL = True
MESH = pl.DeviceIdType.MESH
NT = (((1,), (1,)), ((), ()))


def ext(a, b):
    return ((a + 2) * 5 + b + 2) * DEPTH


def near(a, b):
    return (a + 1) * 3 + b + 1


def plus_shift(d):
    x = d - 2
    return 2 * x + 2 * x * x * x


def dot(a, b):
    return jnp.dot(a, b, preferred_element_type=jnp.float32)


def dot_nt(a, b):
    return lax.dot_general(a, b, NT, preferred_element_type=jnp.float32)


def kernel(
    rows, cols, slots,
    dens, nbrs, pattern,
    out,
    own, row_lo, row_hi, mid_lo, mid_hi, end_lo0, end_lo3, end_hi0, end_hi3,
    diag_ll1, diag_ll2, diag_lh1, diag_lh2, diag_hl1, diag_hl2, diag_hh1, diag_hh2,
    meta_v, meta, lists, tabs_v, tabs, lhs, acc, square, cubed,
    local_sem, meta_sem, tab_send, tab_recv, tab_local,
    row_send, row_recv, mid_send, mid_recv, end_send, end_recv, diag_send, diag_recv,
):
    r = lax.axis_index("row")
    c = lax.axis_index("col")
    size = own.shape[-1]
    row_bufs, mid_bufs, end_bufs = (row_lo, row_hi), (mid_lo, mid_hi), ((end_lo0, end_lo3), (end_hi0, end_hi3))
    diag_bufs = (((diag_ll1, diag_ll2), (diag_lh1, diag_lh2)), ((diag_hl1, diag_hl2), (diag_hh1, diag_hh2)))

    def exists(a, b):
        here = None
        for step, at, count in ((a, r, rows), (b, c, cols)):
            test = at > 0 if step < 0 else at < count - 1
            if step:
                here = test if here is None else jnp.logical_and(here, test)
        return here

    def device(a, b):
        return {"row": r + a, "col": c + b}

    around = [s for s in PLUS + DIAG if s != (0, 0)]
    barrier = pltpu.get_barrier_semaphore()
    for a, b in around:
        @pl.when(exists(a, b))
        def _(a=a, b=b):
            pl.semaphore_signal(barrier, inc=1, device_id=device(a, b), device_id_type=MESH)
    high = (r + 1) // rows
    low = (rows - r) // rows
    right = (c + 1) // cols
    left = (cols - c) // cols
    pl.semaphore_wait(barrier, (3 - high - low) * (3 - right - left) - 1)

    def tab_copy(a, b):
        return pltpu.make_async_remote_copy(
            src_ref=lists.at[4], dst_ref=lists.at[near(-a, -b)],
            send_sem=tab_send.at[near(a, b)], recv_sem=tab_recv.at[near(-a, -b)],
            device_id=device(a, b), device_id_type=MESH)

    def row_copy(side):
        return pltpu.make_async_remote_copy(
            src_ref=dens, dst_ref=row_bufs[side].at[:, pl.ds(0, slots)],
            send_sem=row_send.at[side], recv_sem=row_recv.at[side],
            device_id=device(1 - 2 * side, 0), device_id_type=MESH)

    def mid_copy(side, i):
        return pltpu.make_async_remote_copy(
            src_ref=dens.at[1 + i], dst_ref=mid_bufs[side].at[i, pl.ds(0, slots)],
            send_sem=mid_send.at[side, i], recv_sem=mid_recv.at[side, i],
            device_id=device(0, 1 - 2 * side), device_id_type=MESH)

    def end_copy(side, i):
        return pltpu.make_async_remote_copy(
            src_ref=dens.at[3 * i], dst_ref=end_bufs[side][i].at[0, pl.ds(0, slots)],
            send_sem=end_send.at[side, i], recv_sem=end_recv.at[side, i],
            device_id=device(0, 1 - 2 * side), device_id_type=MESH)

    def diag_copy(side, col_side, i):
        return pltpu.make_async_remote_copy(
            src_ref=mid_bufs[col_side].at[i, pl.ds(0, slots)],
            dst_ref=diag_bufs[side][col_side][i].at[0, pl.ds(0, slots)],
            send_sem=diag_send.at[side, col_side, i], recv_sem=diag_recv.at[side, col_side, i],
            device_id=device(1 - 2 * side, 0), device_id_type=MESH)

    sides = (0, 1)
    lists[4] = jnp.zeros_like(lists[4])
    lists[4, 0:DEPTH, 0:slots] = nbrs[...]
    for a, b in around:
        pl.when(exists(a, b))(lambda a=a, b=b: tab_copy(a, b).start())
    for i in sides:
        for side in sides:
            pl.when(exists(0, 1 - 2 * side))(lambda side=side, i=i: mid_copy(side, i).start())
    for side in sides:
        pl.when(exists(1 - 2 * side, 0))(lambda side=side: row_copy(side).start())
    for i in sides:
        for side in sides:
            pl.when(exists(0, 1 - 2 * side))(lambda side=side, i=i: end_copy(side, i).start())
    load = pltpu.make_async_copy(dens, own.at[:, pl.ds(0, slots)], local_sem)
    load.start()

    def steps(groups):
        known = jnp.maximum(groups, 0)
        cell = jnp.right_shift(known, DEPTH.bit_length() - 1)
        row = jnp.zeros_like(cell)
        for i in range(1, rows):
            row += (cell >= i * cols).astype(jnp.int32)
        return row, cell - row * cols, jnp.bitwise_and(known, DEPTH - 1)

    lanes = lax.broadcasted_iota(jnp.int32, (1, meta_v.shape[2]), 1)

    def slot_table(listed, a, b):
        row, col, p = steps(listed)
        da, db = row - r - a, col - c - b
        corner = 20 + (da + 1) + jnp.right_shift(db + 1, 1)
        q = jnp.where(da * db == 0, (2 + db + 2 * da) * DEPTH + p, corner)
        q = jnp.where(listed >= 0, q, -1)
        table = jnp.full((DEPTH, meta_v.shape[2]), slots, jnp.int32)
        for w in range(slots):
            table = jnp.where(lanes == q[:, w:w + 1], w, table)
        return table, da, db, p

    meta_v[...] = jnp.zeros_like(meta_v)
    tabs_v[...] = jnp.zeros_like(tabs_v)
    listed = nbrs[...]
    present = listed >= 0
    table, da, db, p = slot_table(listed, 0, 0)
    meta_v[0, 0:DEPTH] = table
    meta_v[2, 0:DEPTH, 0:slots] = jnp.clip(
        jnp.where(present, near(da, db) * DEPTH + p, 16), 0, cubed.shape[0] - 1)
    meta_v[3, 0:DEPTH, 0:slots] = jnp.clip(
        jnp.where(present, ext(da, db) + p, ext(0, 0)), 0, square.shape[0] - 1)
    meta_v[4, 0:DEPTH, 0:slots] = present.astype(jnp.int32)
    listed = pattern[...]
    row, col, p = steps(listed)
    kept = jnp.where(listed >= 0, ext(row - r, col - c) + p, -1)
    mask = jnp.zeros((2, meta_v.shape[2]), jnp.int32)
    for i in range(listed.shape[1]):
        mask = jnp.where(lanes == kept[:, i:i + 1], 1, mask)
    meta_v[1, 0:2] = mask
    meta_load = pltpu.make_async_copy(meta_v, meta, meta_sem)
    meta_load.start()
    meta_load.wait()

    blank = jnp.zeros((size, size), own.dtype)
    single = end_bufs + diag_bufs[0] + diag_bufs[1]
    for buf in (own,) + row_bufs + mid_bufs + tuple(b for pair in single for b in pair):
        for i in range(buf.shape[0]):
            buf[i, slots] = blank

    @pl.loop(0, acc.shape[0])
    def _(e):
        acc[e] = jnp.zeros((2 * size, size), jnp.float32)

    for a, b in around:
        @pl.when(exists(a, b))
        def _(a=a, b=b):
            tab_copy(-a, -b).wait_recv()
            tabs_v[near(a, b), 0:DEPTH] = slot_table(lists[near(a, b), 0:DEPTH, 0:slots], a, b)[0]
            copy = pltpu.make_async_copy(
                tabs_v.at[near(a, b)], tabs.at[near(a, b)], tab_local.at[near(a, b)])
            copy.start()
            copy.wait()
    load.wait()

    def held(a, b, l, q):
        slot = meta[0, l, q] if (a, b) == (0, 0) else tabs[near(a, b), l, q]
        if (a, b) == (0, 0):
            return own[l, slot]
        if b == 0:
            return row_bufs[(a + 1) // 2][l, slot]
        if a == 0:
            if l in (1, 2):
                return mid_bufs[(b + 1) // 2][l - 1, slot]
            return end_bufs[(b + 1) // 2][l // 3][0, slot]
        return diag_bufs[(a + 1) // 2][(b + 1) // 2][l - 1][0, slot]

    planes = range(DEPTH)

    def add_plus(a, b, some):
        at = PLUS.index((a, b))
        for i, l in enumerate(some):
            for g in (0, 1):
                lhs[g * size:(g + 1) * size, i * size:(i + 1) * size] = own[
                    g + 1, meta[0, g + 1, at * DEPTH + l]]

        @pl.loop(0, len(PLUS), unroll=UNROLL)
        def _(d):
            right_side = jnp.concatenate([
                jnp.concatenate([held(a, b, l, d * DEPTH + p) for p in planes], axis=1)
                for l in some], axis=0)
            total = dot(lhs[:, :len(some) * size], right_side)
            e = ext(a, b) + plus_shift(d)
            for p in planes:
                acc[e + p] += total[:, p * size:(p + 1) * size]

        for j, l in enumerate(some):
            right_side = jnp.concatenate(
                [held(a, b, l, len(PLUS) * DEPTH + i) for i in range(4)], axis=1)
            total = dot(lhs[:, j * size:(j + 1) * size], right_side)
            for i, (da, db) in enumerate(DIAG):
                acc[ext(a + da, b + db) + l] += total[:, i * size:(i + 1) * size]

    def add_diag(a, b, g):
        at = len(PLUS) * DEPTH + DIAG.index((a, b))
        l = g + 1
        left_side = own[l, meta[0, l, at]]
        half = slice(g * size, (g + 1) * size)

        @pl.loop(0, len(PLUS), unroll=UNROLL)
        def _(d):
            right_side = jnp.concatenate(
                [held(a, b, l, d * DEPTH + p) for p in planes], axis=1)
            total = dot(left_side, right_side)
            e = ext(a, b) + plus_shift(d)
            for p in planes:
                acc[e + p, half] += total[:, p * size:(p + 1) * size]

        right_side = jnp.concatenate(
            [held(a, b, l, len(PLUS) * DEPTH + i) for i in range(4)], axis=1)
        total = dot(left_side, right_side)
        for i, (da, db) in enumerate(DIAG):
            acc[ext(a + da, b + db) + l, half] += total[:, i * size:(i + 1) * size]

    def forward(i):
        for col_side in sides:
            b = 2 * col_side - 1
            pl.when(exists(0, b))(lambda s=col_side: mid_copy(s, i).wait_recv())
            for side in sides:
                pl.when(jnp.logical_and(exists(0, b), exists(1 - 2 * side, 0)))(
                    lambda side=side, s=col_side: diag_copy(side, s, i).start())

    def finish(first, count):
        @pl.loop(0, count, unroll=1 if count % 2 else 2)
        def _(i):
            e = first + i
            for g in (0, 1):
                half = slice(g * size, (g + 1) * size)
                square[e, half] = jnp.where(meta[1, g, e] > 0, acc[e, half], 0.0).astype(square.dtype)

    add_plus(0, 0, planes)
    forward(0)
    forward(1)
    for side in sides:
        a = 2 * side - 1

        @pl.when(exists(a, 0))
        def _(a=a, side=side):
            row_copy(side).wait_recv()
            add_plus(a, 0, planes)
    for side in sides:
        b = 2 * side - 1
        pl.when(exists(0, b))(lambda b=b: add_plus(0, b, (1, 2)))

    def end_part(i):
        for side in sides:
            b = 2 * side - 1

            @pl.when(exists(0, b))
            def _(b=b, side=side):
                end_copy(side, i).wait_recv()
                add_plus(0, b, (3 * i,))

    def diag_part(i):
        for side in sides:
            for col_side in sides:
                a, b = 2 * side - 1, 2 * col_side - 1

                @pl.when(exists(a, b))
                def _(a=a, b=b, side=side, col_side=col_side):
                    diag_copy(side, col_side, i).wait_recv()
                    add_diag(a, b, i)

    diag_part(0)
    end_part(0)
    diag_part(1)
    for a in (-2, 2):
        finish(ext(a, -1), 3 * DEPTH)
        for b in (-2, 2):
            finish(ext(a, b) + 1, 2)
    for a in (-1, 1):
        for b in (-2, 0, 2):
            finish(ext(a, b), 3)
    end_part(1)
    finish(ext(0, -2), 5 * DEPTH)
    for a in (-1, 1):
        for b in (-2, 0, 2):
            finish(ext(a, b) + 3, 1)
        for b in (-1, 1):
            finish(ext(a, b), DEPTH)

    def cube_plus(a, b):
        first = near(a, b) * DEPTH
        for l in planes:
            left_side = jnp.concatenate(
                [square[ext(a + da, b + db) + l] for da, db in DIAG], axis=1)
            right_side = jnp.concatenate(
                [held(a, b, l, len(PLUS) * DEPTH + i) for i in range(4)], axis=1)
            cubed[first + l] = dot_nt(left_side, right_side)

        @pl.loop(0, len(PLUS), unroll=UNROLL)
        def _(d):
            e = ext(a, b) + plus_shift(d)
            left_side = jnp.concatenate([square[e + p] for p in planes], axis=1)
            right_side = jnp.concatenate([
                jnp.concatenate([held(a, b, l, d * DEPTH + p) for p in planes], axis=1)
                for l in planes], axis=0)
            total = dot_nt(left_side, right_side)
            for l in planes:
                cubed[first + l] += total[:, l * size:(l + 1) * size]

    def cube_diag(a, b):
        for g in (0, 1):
            l = g + 1
            half = slice(g * size, (g + 1) * size)
            left_side = jnp.concatenate(
                [square[ext(a + da, b + db) + l, half] for da, db in DIAG]
                + [square[ext(a + da, b + db) + p, half] for da, db in PLUS for p in planes], axis=1)
            places = [len(PLUS) * DEPTH + i for i in range(4)] + list(range(len(PLUS) * DEPTH))
            right_side = jnp.concatenate([held(a, b, l, q) for q in places], axis=1)
            cubed[near(a, b) * DEPTH + l, half] = dot_nt(left_side, right_side)

    cube_plus(0, 0)
    for a, b in around:
        pl.when(exists(a, b))(
            lambda a=a, b=b: cube_diag(a, b) if a and b else cube_plus(a, b))

    @pl.loop(0, slots, unroll=1)
    def _(w):
        for g in (0, 1):
            half = slice(g * size, (g + 1) * size)
            updated = (3.0 * square[meta[3, g + 1, w], half].astype(jnp.float32)
                       - 2.0 * cubed[meta[2, g + 1, w], half])
            out[g, w] = jnp.where(meta[4, g + 1, w] > 0, updated, 0.0).astype(out.dtype)

    for a, b in around:
        pl.when(exists(a, b))(lambda a=a, b=b: tab_copy(a, b).wait_send())
    for side in sides:
        pl.when(exists(1 - 2 * side, 0))(lambda side=side: row_copy(side).wait_send())
        for i in sides:
            pl.when(exists(0, 1 - 2 * side))(lambda side=side, i=i: mid_copy(side, i).wait_send())
            pl.when(exists(0, 1 - 2 * side))(lambda side=side, i=i: end_copy(side, i).wait_send())
            for s in sides:
                pl.when(jnp.logical_and(exists(0, 2 * s - 1), exists(1 - 2 * side, 0)))(
                    lambda side=side, s=s, i=i: diag_copy(side, s, i).wait_send())


def shards(rows, cols, density, neighbours, square_pattern):
    density, neighbours, square_pattern = density[0, 0], neighbours[0, 0], square_pattern[0, 0]
    slots, size = density.shape[1], density.shape[2]
    block = (size, size)
    dma = pltpu.SemaphoreType.DMA
    bf16 = density.dtype

    def buf(n):
        return pltpu.VMEM((n, slots + 1) + block, bf16)

    purified = pl.pallas_call(
        functools.partial(kernel, rows, cols, slots),
        out_shape=jax.ShapeDtypeStruct((2, slots) + block, bf16),
        in_specs=[pl.BlockSpec(memory_space=pl.ANY)] + [pl.BlockSpec(memory_space=pltpu.VMEM)] * 2,
        out_specs=pl.BlockSpec(memory_space=pltpu.VMEM),
        scratch_shapes=[
            buf(4), buf(4), buf(4), buf(2), buf(2),
            *[buf(1)] * 12,
            pltpu.VMEM((5, 8, 128), jnp.int32),
            pltpu.SMEM((5, 8, 128), jnp.int32),
            pltpu.VMEM((9, 8, 128), jnp.int32),
            pltpu.VMEM((9, 8, 128), jnp.int32),
            pltpu.SMEM((9, 8, 128), jnp.int32),
            pltpu.VMEM((2 * size, DEPTH * size), bf16),
            pltpu.VMEM((100, 2 * size, size), jnp.float32),
            pltpu.VMEM((100, 2 * size, size), bf16),
            pltpu.VMEM((36, 2 * size, size), jnp.float32),
            dma, dma, dma((9,)), dma((9,)), dma((9,)),
            dma((2,)), dma((2,)), dma((2, 2)), dma((2, 2)), dma((2, 2)), dma((2, 2)),
            dma((2, 2, 2)), dma((2, 2, 2)),
        ],
        compiler_params=pltpu.CompilerParams(
            collective_id=0, has_side_effects=True, vmem_limit_bytes=56 * 1024 * 1024),
        cost_estimate=pl.CostEstimate(flops=6 * 10**9, bytes_accessed=20 * 10**6, transcendentals=0),
    )(density, neighbours, square_pattern)
    return purified[None, None]


def solution(mesh):
    in_specs = (
        P("row", "col", "sys", None, None, None),
        P("row", "col", "sys", None),
        P("row", "col", "sys", None),
    )
    out_specs = P("row", "col", "sys", None, None, None)
    body = functools.partial(shards, mesh.shape["row"], mesh.shape["col"])
    return jax.shard_map(body, mesh=mesh, in_specs=in_specs, out_specs=out_specs, check_vma=False)
```

```python
import functools

import jax
import jax.numpy as jnp
from jax import lax
from jax.experimental import pallas as pl
from jax.experimental.pallas import tpu as pltpu
from jax.sharding import PartitionSpec as P

PLUS = ((-1, 0), (0, -1), (0, 0), (0, 1), (1, 0))
DIAG = ((-1, -1), (-1, 1), (1, -1), (1, 1))
DEPTH = 4
UNROLL = True
MESH = pl.DeviceIdType.MESH
NT = (((1,), (1,)), ((), ()))


def ext(a, b):
    return ((a + 2) * 5 + b + 2) * DEPTH


def near(a, b):
    return (a + 1) * 3 + b + 1


def plus_shift(d):
    x = d - 2
    return 2 * x + 2 * x * x * x


def dot(a, b):
    return jnp.dot(a, b, preferred_element_type=jnp.float32)


def dot_nt(a, b):
    return lax.dot_general(a, b, NT, preferred_element_type=jnp.float32)


def kernel(
    rows, cols, slots,
    dens, nbrs, pattern,
    out,
    own, row_lo, row_hi, mid_lo, mid_hi, end_lo0, end_lo3, end_hi0, end_hi3,
    diag_ll1, diag_ll2, diag_lh1, diag_lh2, diag_hl1, diag_hl2, diag_hh1, diag_hh2,
    meta_v, meta, lists, tabs_v, tabs, lhs, acc, square, cubed,
    local_sem, meta_sem, tab_send, tab_recv, tab_local,
    row_send, row_recv, mid_send, mid_recv, end_send, end_recv, diag_send, diag_recv,
):
    r = lax.axis_index("row")
    c = lax.axis_index("col")
    size = own.shape[-1]
    row_bufs, mid_bufs, end_bufs = (row_lo, row_hi), (mid_lo, mid_hi), ((end_lo0, end_lo3), (end_hi0, end_hi3))
    diag_bufs = (((diag_ll1, diag_ll2), (diag_lh1, diag_lh2)), ((diag_hl1, diag_hl2), (diag_hh1, diag_hh2)))

    def exists(a, b):
        here = None
        for step, at, count in ((a, r, rows), (b, c, cols)):
            test = at > 0 if step < 0 else at < count - 1
            if step:
                here = test if here is None else jnp.logical_and(here, test)
        return here

    def device(a, b):
        return {"row": r + a, "col": c + b}

    around = [s for s in PLUS + DIAG if s != (0, 0)]
    barrier = pltpu.get_barrier_semaphore()
    for a, b in around:
        @pl.when(exists(a, b))
        def _(a=a, b=b):
            pl.semaphore_signal(barrier, inc=1, device_id=device(a, b), device_id_type=MESH)
    high = (r + 1) // rows
    low = (rows - r) // rows
    right = (c + 1) // cols
    left = (cols - c) // cols
    pl.semaphore_wait(barrier, (3 - high - low) * (3 - right - left) - 1)

    def tab_copy(a, b):
        return pltpu.make_async_remote_copy(
            src_ref=lists.at[4], dst_ref=lists.at[near(-a, -b)],
            send_sem=tab_send.at[near(a, b)], recv_sem=tab_recv.at[near(-a, -b)],
            device_id=device(a, b), device_id_type=MESH)

    def row_copy(side):
        return pltpu.make_async_remote_copy(
            src_ref=dens, dst_ref=row_bufs[side].at[:, pl.ds(0, slots)],
            send_sem=row_send.at[side], recv_sem=row_recv.at[side],
            device_id=device(1 - 2 * side, 0), device_id_type=MESH)

    def mid_copy(side, i):
        return pltpu.make_async_remote_copy(
            src_ref=dens.at[1 + i], dst_ref=mid_bufs[side].at[i, pl.ds(0, slots)],
            send_sem=mid_send.at[side, i], recv_sem=mid_recv.at[side, i],
            device_id=device(0, 1 - 2 * side), device_id_type=MESH)

    def end_copy(side, i):
        return pltpu.make_async_remote_copy(
            src_ref=dens.at[3 * i], dst_ref=end_bufs[side][i].at[0, pl.ds(0, slots)],
            send_sem=end_send.at[side, i], recv_sem=end_recv.at[side, i],
            device_id=device(0, 1 - 2 * side), device_id_type=MESH)

    def diag_copy(side, col_side, i):
        return pltpu.make_async_remote_copy(
            src_ref=mid_bufs[col_side].at[i, pl.ds(0, slots)],
            dst_ref=diag_bufs[side][col_side][i].at[0, pl.ds(0, slots)],
            send_sem=diag_send.at[side, col_side, i], recv_sem=diag_recv.at[side, col_side, i],
            device_id=device(1 - 2 * side, 0), device_id_type=MESH)

    sides = (0, 1)
    lists[4] = jnp.zeros_like(lists[4])
    lists[4, 0:DEPTH, 0:slots] = nbrs[...]
    for a, b in around:
        pl.when(exists(a, b))(lambda a=a, b=b: tab_copy(a, b).start())
    for i in sides:
        for side in sides:
            pl.when(exists(0, 1 - 2 * side))(lambda side=side, i=i: mid_copy(side, i).start())
    for side in sides:
        pl.when(exists(1 - 2 * side, 0))(lambda side=side: row_copy(side).start())
    for i in sides:
        for side in sides:
            pl.when(exists(0, 1 - 2 * side))(lambda side=side, i=i: end_copy(side, i).start())
    load = pltpu.make_async_copy(dens, own.at[:, pl.ds(0, slots)], local_sem)
    load.start()

    def steps(groups):
        known = jnp.maximum(groups, 0)
        cell = jnp.right_shift(known, DEPTH.bit_length() - 1)
        row = jnp.zeros_like(cell)
        for i in range(1, rows):
            row += (cell >= i * cols).astype(jnp.int32)
        return row, cell - row * cols, jnp.bitwise_and(known, DEPTH - 1)

    lanes = lax.broadcasted_iota(jnp.int32, (1, meta_v.shape[2]), 1)

    def slot_table(listed, a, b):
        row, col, p = steps(listed)
        da, db = row - r - a, col - c - b
        corner = 20 + (da + 1) + jnp.right_shift(db + 1, 1)
        q = jnp.where(da * db == 0, (2 + db + 2 * da) * DEPTH + p, corner)
        q = jnp.where(listed >= 0, q, -1)
        table = jnp.full((DEPTH, meta_v.shape[2]), slots, jnp.int32)
        for w in range(slots):
            table = jnp.where(lanes == q[:, w:w + 1], w, table)
        return table, da, db, p

    meta_v[...] = jnp.zeros_like(meta_v)
    tabs_v[...] = jnp.zeros_like(tabs_v)
    listed = nbrs[...]
    present = listed >= 0
    table, da, db, p = slot_table(listed, 0, 0)
    meta_v[0, 0:DEPTH] = table
    meta_v[2, 0:DEPTH, 0:slots] = jnp.clip(
        jnp.where(present, near(da, db) * DEPTH + p, 16), 0, cubed.shape[0] - 1)
    meta_v[3, 0:DEPTH, 0:slots] = jnp.clip(
        jnp.where(present, ext(da, db) + p, ext(0, 0)), 0, square.shape[0] - 1)
    meta_v[4, 0:DEPTH, 0:slots] = present.astype(jnp.int32)
    listed = pattern[...]
    row, col, p = steps(listed)
    kept = jnp.where(listed >= 0, ext(row - r, col - c) + p, -1)
    mask = jnp.zeros((2, meta_v.shape[2]), jnp.int32)
    for i in range(listed.shape[1]):
        mask = jnp.where(lanes == kept[:, i:i + 1], 1, mask)
    meta_v[1, 0:2] = mask
    meta_load = pltpu.make_async_copy(meta_v, meta, meta_sem)
    meta_load.start()
    meta_load.wait()

    blank = jnp.zeros((size, size), own.dtype)
    single = end_bufs + diag_bufs[0] + diag_bufs[1]
    for buf in (own,) + row_bufs + mid_bufs + tuple(b for pair in single for b in pair):
        for i in range(buf.shape[0]):
            buf[i, slots] = blank

    @pl.loop(0, acc.shape[0])
    def _(e):
        acc[e] = jnp.zeros((2 * size, size), jnp.float32)

    for a, b in around:
        @pl.when(exists(a, b))
        def _(a=a, b=b):
            tab_copy(-a, -b).wait_recv()
            tabs_v[near(a, b), 0:DEPTH] = slot_table(lists[near(a, b), 0:DEPTH, 0:slots], a, b)[0]
            copy = pltpu.make_async_copy(
                tabs_v.at[near(a, b)], tabs.at[near(a, b)], tab_local.at[near(a, b)])
            copy.start()
            copy.wait()
    load.wait()

    def held(a, b, l, q):
        slot = meta[0, l, q] if (a, b) == (0, 0) else tabs[near(a, b), l, q]
        if (a, b) == (0, 0):
            return own[l, slot]
        if b == 0:
            return row_bufs[(a + 1) // 2][l, slot]
        if a == 0:
            if l in (1, 2):
                return mid_bufs[(b + 1) // 2][l - 1, slot]
            return end_bufs[(b + 1) // 2][l // 3][0, slot]
        return diag_bufs[(a + 1) // 2][(b + 1) // 2][l - 1][0, slot]

    planes = range(DEPTH)

    def add_plus(a, b, some):
        at = PLUS.index((a, b))
        for i, l in enumerate(some):
            for g in (0, 1):
                lhs[g * size:(g + 1) * size, i * size:(i + 1) * size] = own[
                    g + 1, meta[0, g + 1, at * DEPTH + l]]

        @pl.loop(0, len(PLUS), unroll=UNROLL)
        def _(d):
            right_side = jnp.concatenate([
                jnp.concatenate([held(a, b, l, d * DEPTH + p) for p in planes], axis=1)
                for l in some], axis=0)
            total = dot(lhs[:, :len(some) * size], right_side)
            e = ext(a, b) + plus_shift(d)
            for p in planes:
                acc[e + p] += total[:, p * size:(p + 1) * size]

        for j, l in enumerate(some):
            right_side = jnp.concatenate(
                [held(a, b, l, len(PLUS) * DEPTH + i) for i in range(4)], axis=1)
            total = dot(lhs[:, j * size:(j + 1) * size], right_side)
            for i, (da, db) in enumerate(DIAG):
                acc[ext(a + da, b + db) + l] += total[:, i * size:(i + 1) * size]

    def add_diag(a, b, g):
        at = len(PLUS) * DEPTH + DIAG.index((a, b))
        l = g + 1
        left_side = own[l, meta[0, l, at]]
        half = slice(g * size, (g + 1) * size)

        @pl.loop(0, len(PLUS), unroll=UNROLL)
        def _(d):
            right_side = jnp.concatenate(
                [held(a, b, l, d * DEPTH + p) for p in planes], axis=1)
            total = dot(left_side, right_side)
            e = ext(a, b) + plus_shift(d)
            for p in planes:
                acc[e + p, half] += total[:, p * size:(p + 1) * size]

        right_side = jnp.concatenate(
            [held(a, b, l, len(PLUS) * DEPTH + i) for i in range(4)], axis=1)
        total = dot(left_side, right_side)
        for i, (da, db) in enumerate(DIAG):
            acc[ext(a + da, b + db) + l, half] += total[:, i * size:(i + 1) * size]

    def forward(i):
        for col_side in sides:
            b = 2 * col_side - 1
            pl.when(exists(0, b))(lambda s=col_side: mid_copy(s, i).wait_recv())
            for side in sides:
                pl.when(jnp.logical_and(exists(0, b), exists(1 - 2 * side, 0)))(
                    lambda side=side, s=col_side: diag_copy(side, s, i).start())

    def finish(first, count):
        @pl.loop(0, count, unroll=1 if count % 4 else 4)
        def _(i):
            e = first + i
            for g in (0, 1):
                half = slice(g * size, (g + 1) * size)
                square[e, half] = jnp.where(meta[1, g, e] > 0, acc[e, half], 0.0).astype(square.dtype)

    add_plus(0, 0, planes)
    forward(0)
    forward(1)
    for side in sides:
        a = 2 * side - 1

        @pl.when(exists(a, 0))
        def _(a=a, side=side):
            row_copy(side).wait_recv()
            add_plus(a, 0, planes)
    for side in sides:
        b = 2 * side - 1
        pl.when(exists(0, b))(lambda b=b: add_plus(0, b, (1, 2)))

    def end_part(i):
        for side in sides:
            b = 2 * side - 1

            @pl.when(exists(0, b))
            def _(b=b, side=side):
                end_copy(side, i).wait_recv()
                add_plus(0, b, (3 * i,))

    def diag_part(i):
        for side in sides:
            for col_side in sides:
                a, b = 2 * side - 1, 2 * col_side - 1

                @pl.when(exists(a, b))
                def _(a=a, b=b, side=side, col_side=col_side):
                    diag_copy(side, col_side, i).wait_recv()
                    add_diag(a, b, i)

    diag_part(0)
    end_part(0)
    diag_part(1)
    for a in (-2, 2):
        finish(ext(a, -1), 3 * DEPTH)
        for b in (-2, 2):
            finish(ext(a, b) + 1, 2)
    for a in (-1, 1):
        for b in (-2, 0, 2):
            finish(ext(a, b), 3)
    end_part(1)
    finish(ext(0, -2), 5 * DEPTH)
    for a in (-1, 1):
        for b in (-2, 0, 2):
            finish(ext(a, b) + 3, 1)
        for b in (-1, 1):
            finish(ext(a, b), DEPTH)

    def cube_plus(a, b):
        first = near(a, b) * DEPTH
        for l in planes:
            left_side = jnp.concatenate(
                [square[ext(a + da, b + db) + l] for da, db in DIAG], axis=1)
            right_side = jnp.concatenate(
                [held(a, b, l, len(PLUS) * DEPTH + i) for i in range(4)], axis=1)
            cubed[first + l] = dot_nt(left_side, right_side)

        @pl.loop(0, len(PLUS), unroll=UNROLL)
        def _(d):
            e = ext(a, b) + plus_shift(d)
            left_side = jnp.concatenate([square[e + p] for p in planes], axis=1)
            right_side = jnp.concatenate([
                jnp.concatenate([held(a, b, l, d * DEPTH + p) for p in planes], axis=1)
                for l in planes], axis=0)
            total = dot_nt(left_side, right_side)
            for l in planes:
                cubed[first + l] += total[:, l * size:(l + 1) * size]

    def cube_diag(a, b):
        for g in (0, 1):
            l = g + 1
            half = slice(g * size, (g + 1) * size)
            left_side = jnp.concatenate(
                [square[ext(a + da, b + db) + l, half] for da, db in DIAG]
                + [square[ext(a + da, b + db) + p, half] for da, db in PLUS for p in planes], axis=1)
            places = [len(PLUS) * DEPTH + i for i in range(4)] + list(range(len(PLUS) * DEPTH))
            right_side = jnp.concatenate([held(a, b, l, q) for q in places], axis=1)
            cubed[near(a, b) * DEPTH + l, half] = dot_nt(left_side, right_side)

    cube_plus(0, 0)
    for a, b in around:
        pl.when(exists(a, b))(
            lambda a=a, b=b: cube_diag(a, b) if a and b else cube_plus(a, b))

    @pl.loop(0, slots, unroll=True)
    def _(w):
        for g in (0, 1):
            half = slice(g * size, (g + 1) * size)
            updated = (3.0 * square[meta[3, g + 1, w], half].astype(jnp.float32)
                       - 2.0 * cubed[meta[2, g + 1, w], half])
            out[g, w] = jnp.where(meta[4, g + 1, w] > 0, updated, 0.0).astype(out.dtype)

    for a, b in around:
        pl.when(exists(a, b))(lambda a=a, b=b: tab_copy(a, b).wait_send())
    for side in sides:
        pl.when(exists(1 - 2 * side, 0))(lambda side=side: row_copy(side).wait_send())
        for i in sides:
            pl.when(exists(0, 1 - 2 * side))(lambda side=side, i=i: mid_copy(side, i).wait_send())
            pl.when(exists(0, 1 - 2 * side))(lambda side=side, i=i: end_copy(side, i).wait_send())
            for s in sides:
                pl.when(jnp.logical_and(exists(0, 2 * s - 1), exists(1 - 2 * side, 0)))(
                    lambda side=side, s=s, i=i: diag_copy(side, s, i).wait_send())


def shards(rows, cols, density, neighbours, square_pattern):
    density, neighbours, square_pattern = density[0, 0], neighbours[0, 0], square_pattern[0, 0]
    slots, size = density.shape[1], density.shape[2]
    block = (size, size)
    dma = pltpu.SemaphoreType.DMA
    bf16 = density.dtype

    def buf(n):
        return pltpu.VMEM((n, slots + 1) + block, bf16)

    purified = pl.pallas_call(
        functools.partial(kernel, rows, cols, slots),
        out_shape=jax.ShapeDtypeStruct((2, slots) + block, bf16),
        in_specs=[pl.BlockSpec(memory_space=pl.ANY)] + [pl.BlockSpec(memory_space=pltpu.VMEM)] * 2,
        out_specs=pl.BlockSpec(memory_space=pltpu.VMEM),
        scratch_shapes=[
            buf(4), buf(4), buf(4), buf(2), buf(2),
            *[buf(1)] * 12,
            pltpu.VMEM((5, 8, 128), jnp.int32),
            pltpu.SMEM((5, 8, 128), jnp.int32),
            pltpu.VMEM((9, 8, 128), jnp.int32),
            pltpu.VMEM((9, 8, 128), jnp.int32),
            pltpu.SMEM((9, 8, 128), jnp.int32),
            pltpu.VMEM((2 * size, DEPTH * size), bf16),
            pltpu.VMEM((100, 2 * size, size), jnp.float32),
            pltpu.VMEM((100, 2 * size, size), bf16),
            pltpu.VMEM((36, 2 * size, size), jnp.float32),
            dma, dma, dma((9,)), dma((9,)), dma((9,)),
            dma((2,)), dma((2,)), dma((2, 2)), dma((2, 2)), dma((2, 2)), dma((2, 2)),
            dma((2, 2, 2)), dma((2, 2, 2)),
        ],
        compiler_params=pltpu.CompilerParams(
            collective_id=0, has_side_effects=True, vmem_limit_bytes=56 * 1024 * 1024),
        cost_estimate=pl.CostEstimate(flops=6 * 10**9, bytes_accessed=20 * 10**6, transcendentals=0),
    )(density, neighbours, square_pattern)
    return purified[None, None]


def solution(mesh):
    in_specs = (
        P("row", "col", "sys", None, None, None),
        P("row", "col", "sys", None),
        P("row", "col", "sys", None),
    )
    out_specs = P("row", "col", "sys", None, None, None)
    body = functools.partial(shards, mesh.shape["row"], mesh.shape["col"])
    return jax.shard_map(body, mesh=mesh, in_specs=in_specs, out_specs=out_specs, check_vma=False)
```
